256 devices in a mesh: head: 8 (over z), rep: 32 (over x, y, core).
Axes of the slice: x: 4, y: 4, z: 8, core: 2. Of those that a mesh axis runs over, the one named last changes fastest.
Arguments:
- trainer_rows: bfloat16 [8, 32, 8, 8, 1024], P('head', 'rep'), may hold values from -2.5 to 2.5
- route: int32 [8, 32, 8, 2], replicated, may hold values from 0 to 2040, as said below
Outputs:
- absorbed_values: bfloat16 [64, 1536, 512], P('head')
- absorbed_scales: bfloat16 [64, 12, 4], P('head')
The draws below stay inside these ranges and needn't reach their ends.
Inputs may be any that keep to these rules, and one draw needn't show every extreme that they name: route[i, j, s] holds the owner group (first entry) and the row offset (second entry) of slot s of the trainer shard on head index i and replica j. The owner groups of one shard's 8 slots are all different; for each owner group the offsets of its 256 slots are the multiples of 8 below 2048, each once.
All inputs are finite; a program needn't handle non-finite values. Where the reference program divides by a largest or mean magnitude, that divisor is 1e-20 or more.
Results may differ from the reference program's by a relative error of at most 0.013.
Values may be sent and summed in bfloat16 or wider, within the bound.
No kernel may reach another device: no remote copies, remote signals or barrier semaphores. Data moves between devices by JAX's collectives and lax.ppermute only.
A program may use at most 128 MiB of HBM per device.

```python
import jax
import jax.numpy as jnp
from jax import lax

QR = 1536
KR = 512
DH = 128
H_DEV = 8
QB = 128
HEADS = 64
LAT = 2048
SHARDS = 256
SROWS = 8
N_HEAD = 8
N_REP = 32


def draw_route(key, part):
    key = jax.random.fold_in(key, 11)
    first_key, second_key = jax.random.split(key)
    device_keys = jax.random.split(first_key, N_HEAD * N_REP)
    owners = jax.vmap(lambda sub_key: jax.random.permutation(sub_key, N_HEAD))(device_keys)
    group_keys = jax.random.split(second_key, N_HEAD)
    block_ids = jax.vmap(lambda sub_key: jax.random.permutation(sub_key, SHARDS))(group_keys)
    device = jnp.arange(SHARDS)[:, None]
    offsets = block_ids[owners, device] * SROWS
    stacked = jnp.stack([owners, offsets], -1).astype(jnp.int32)
    return stacked.reshape(N_HEAD, N_REP, N_HEAD, 2)


def steps_of(own_key, shape, cuts, least, high):
    def one(position, shards_of):
        steps = jax.random.uniform(jax.random.fold_in(jax.random.fold_in(own_key, 6), position), (shards_of,), jnp.float32, least / len(cuts), high / len(cuts))
        return jnp.repeat(jnp.exp(steps), shape[position] // shards_of).reshape((-1,) + (1,) * (len(shape) - position - 1))

    level = one(*cuts[0])
    for cut in cuts[1:]:
        level = level * one(*cut)
    return level


def normal_values(rng, extent, scale, reach, cuts=(), kind=jnp.bfloat16):
    entries = jax.random.normal(rng, extent, jnp.float32) * scale
    if len(cuts) > 0:
        entries = steps_of(rng, extent, cuts, -0.22, 0.18) * entries
    return jnp.clip(entries, min=-reach, max=reach).astype(kind)


def setup_inputs(seed: int = 0) -> dict:
    seeds = jax.random.split(jax.random.key(seed), 3)
    trainer_rows = normal_values(seeds[0], (N_HEAD, N_REP, N_HEAD, SROWS, H_DEV * DH), 0.3, 2.5, ((0, 8), (1, 32)))
    route = draw_route(jax.random.fold_in(seeds[2], 71), 0)
    return dict(trainer_rows=trainer_rows, route=route)


EPSILON = 1e-6


def absorb(query_part, key_part):
    products = jnp.einsum("qhd,khd->hqk", query_part.astype(jnp.float32), key_part.astype(jnp.float32))
    head_count, row_count, col_count = products.shape
    tiled = products.reshape(head_count, row_count // QB, QB, col_count // QB, QB)
    scales = (jnp.max(jnp.abs(tiled), axis=(2, 4)) + EPSILON).astype(jnp.bfloat16)
    values = (tiled / scales.astype(jnp.float32)[:, :, None, :, None]).astype(jnp.bfloat16)
    return values.reshape(head_count, row_count, col_count), scales


def reference(trainer_rows, route):
    shards = trainer_rows.reshape(SHARDS * N_HEAD, SROWS, H_DEV * DH)
    owners = route[..., 0].reshape(-1).astype(jnp.int32)
    offsets = route[..., 1].reshape(-1).astype(jnp.int32)
    blocks = jnp.zeros((N_HEAD, LAT // SROWS, SROWS, H_DEV * DH), trainer_rows.dtype)
    blocks = blocks.at[owners, offsets // SROWS].set(shards)
    factors = blocks.reshape(N_HEAD, LAT, H_DEV, DH)

    def one_group(stacked):
        return absorb(stacked[:QR], stacked[QR:])

    values, scales = lax.map(one_group, factors)
    return values.reshape(HEADS, QR, KR), scales.reshape(HEADS, QR // QB, KR // QB)
```

```python
import functools

import jax
import jax.numpy as jnp
from jax import lax
from jax.experimental import pallas as pl
from jax.experimental.pallas import tpu as pltpu
from jax.sharding import PartitionSpec as P

QR = 1536
KR = 512
DH = 128
H_DEV = 8
QB = 128
LAT = QR + KR
NZ = 8
NX = 4
NY = 4
NC = 2
HALF = H_DEV // NC
WIDE = HALF * DH
EPSILON = 1e-06
AXES = ("head", "rep")


def index_of(z, x, y, c):
    return (z % NZ) * (NX * NY * NC) + (x % NX) * (NY * NC) + (y % NY) * NC + c


def every():
    return [
        (z, x, y, c)
        for z in range(NZ)
        for x in range(NX)
        for y in range(NY)
        for c in range(NC)
    ]


def pairs(target):
    return [(index_of(*d), index_of(*target(*d))) for d in every()]


def first_axis(k):
    return pairs(lambda z, x, y, c: (z, x - k, y, c) if c == 0 else (z, x, y - k, c))


def second_axis(k):
    return pairs(lambda z, x, y, c: (z, x, y - k, c) if c == 0 else (z, x - k, y, c))


def other_core():
    return pairs(lambda z, x, y, c: (z, x, y, 1 - c))


def columns():
    return [
        [index_of(z, x, y, c) for z in range(NZ) for c in range(NC)]
        for x in range(NX)
        for y in range(NY)
    ]


def absorb_kernel(swapped, meta, rows, b0, b1, b2, b3, *refs):
    values, scales, placed = refs[-3:]
    step = pl.program_id(0)

    @pl.when(step == 0)
    def _():
        swap = meta[0] if not swapped else 1 - meta[0]
        at_x, at_y = meta[1], meta[2]
        for second, blocks in enumerate((b0, b1, b2, b3)):

            def body(first, carry, second=second, blocks=blocks):
                x = (at_x + jnp.where(swap == 1, second, first)) & (NX - 1)
                y = (at_y + jnp.where(swap == 1, first, second)) & (NY - 1)
                for z in range(NZ):
                    for c in range(NC):
                        row = pl.multiple_of(rows[z, x * (NY * NC) + y * NC + c], 8)
                        block = blocks[first * (NZ * NC) + z * NC + c].astype(jnp.float32)
                        for h in range(HALF):
                            placed[h, pl.ds(row, 8), :] = block[:, h * DH : (h + 1) * DH]
                return carry

            lax.fori_loop(0, NX, body, 0)

    key = placed[step, QR:, :].astype(jnp.bfloat16)
    row_at = lax.broadcasted_iota(jnp.int32, (4, 128), 0)
    col_at = lax.broadcasted_iota(jnp.int32, (4, 128), 1)
    table = jnp.zeros((4, 128), jnp.float32)
    for i in range(QR // QB):
        query = placed[step, i * QB : (i + 1) * QB, :].astype(jnp.bfloat16)
        product = lax.dot_general(
            query, key, (((1,), (1,)), ((), ())), preferred_element_type=jnp.float32
        )
        for j in range(KR // QB):
            block = product[:, j * QB : (j + 1) * QB]
            peak = jnp.max(jnp.abs(block), axis=(0, 1), keepdims=True)
            scale = (peak + EPSILON).astype(jnp.bfloat16).astype(jnp.float32)
            values[0, i * QB : (i + 1) * QB, j * QB : (j + 1) * QB] = (
                block * (1.0 / scale)
            ).astype(jnp.bfloat16)
            table = jnp.where((row_at == j) & (col_at == i), scale, table)
    scales[0] = table[:, : QR // QB].astype(jnp.bfloat16)


def absorb(meta, rows, blocks, earlier=None):
    swapped = earlier is not None

    def head(step, meta, rows):
        half = 1 - meta[0] if swapped else meta[0]
        return (half * HALF + step, 0, 0)

    whole = pl.BlockSpec((NX * NZ * NC, 8, WIDE), lambda step, meta, rows: (0, 0, 0))
    anywhere = pl.BlockSpec(memory_space=pl.ANY)
    return pl.pallas_call(
        functools.partial(absorb_kernel, swapped),
        out_shape=(
            jax.ShapeDtypeStruct((H_DEV, QR, KR), jnp.bfloat16),
            jax.ShapeDtypeStruct((H_DEV, KR // QB, QR // QB), jnp.bfloat16),
        ),
        grid_spec=pltpu.PrefetchScalarGridSpec(
            num_scalar_prefetch=2,
            grid=(HALF,),
            in_specs=[whole] * 4 + ([anywhere] * 2 if swapped else []),
            out_specs=(
                pl.BlockSpec((1, QR, KR), head),
                pl.BlockSpec((1, KR // QB, QR // QB), head),
            ),
            scratch_shapes=[pltpu.VMEM((HALF, LAT, DH), jnp.float32)],
        ),
        input_output_aliases={6: 0, 7: 1} if swapped else {},
        compiler_params=pltpu.CompilerParams(vmem_limit_bytes=32 * 2**20),
        cost_estimate=pl.CostEstimate(
            flops=2 * HALF * QR * KR * DH,
            bytes_accessed=HALF * QR * KR * 2 + LAT * WIDE * 2,
            transcendentals=0,
        ),
    )(meta, rows, *blocks, *(earlier or ()))


def gather_phase(block, target):
    return [block] + [lax.ppermute(block, AXES, target(k)) for k in (1, 2, 3)]


def on_device(trainer_rows, route):
    group = lax.axis_index("head")
    replica = lax.axis_index("rep")
    held = trainer_rows[0, 0]
    owners = lax.dynamic_slice(
        route, (group, replica, 0, 0), (1, 1, NZ, 1)
    ).reshape(NZ)
    chosen = owners[None, :] == jnp.arange(NZ, dtype=jnp.int32)[:, None]
    picks = jnp.sum(jnp.where(chosen, jnp.arange(NZ, dtype=jnp.int32)[None], 0), axis=1)
    ordered = held[picks].reshape(NZ, 8, NC, WIDE).transpose(0, 2, 1, 3)
    mine = route[:, :, :, 0] == group
    rows = jnp.sum(jnp.where(mine, route[:, :, :, 1], 0), axis=2)
    meta = jnp.stack([replica % NC, replica // (NY * NC), replica // NC % NY])
    arrived = lax.all_to_all(
        ordered.reshape(NZ * NC, 8, WIDE),
        AXES,
        split_axis=0,
        concat_axis=0,
        axis_index_groups=columns(),
        tiled=True,
    )
    line = jnp.concatenate(gather_phase(arrived, first_axis))
    own = gather_phase(line, second_axis)
    other = [lax.ppermute(b, AXES, other_core()) for b in own]
    earlier = absorb(meta, rows, own)
    values, scales = absorb(meta, rows, other, earlier)
    return values, scales.transpose(0, 2, 1)


def solution(mesh):
    return jax.shard_map(
        on_device,
        mesh=mesh,
        in_specs=(P("head", "rep", None, None, None), P()),
        out_specs=(P("head", None, None), P("head", None, None)),
        check_vma=False,
    )
```

```python
import jax
import jax.numpy as jnp
from jax import lax
from jax.experimental import pallas as pl
from jax.experimental.pallas import tpu as pltpu
from jax.sharding import PartitionSpec as P

QR = 1536
KR = 512
DH = 128
H_DEV = 8
QB = 128
LAT = QR + KR
NZ = 8
NX = 4
NY = 4
NC = 2
STEPS = NZ // NC
Q_BLOCKS = QR // QB
K_BLOCKS = KR // QB
SEND = 4
HALF = H_DEV // 2
WIDE = HALF * DH
EPSILON = 1e-06
AXES = ("head", "rep")


def index_of(z, x, y, c):
    return (z % NZ) * (NX * NY * NC) + (x % NX) * (NY * NC) + (y % NY) * NC + c


def pairs(target):
    every = [
        (z, x, y, c)
        for z in range(NZ)
        for x in range(NX)
        for y in range(NY)
        for c in range(NC)
    ]
    return [(index_of(*d), index_of(*target(*d))) for d in every]


def z_shift(core, step):
    if core == 0:
        return step
    return -step if step else NZ // 2


def along_z(step):
    return pairs(lambda z, x, y, c: (z + z_shift(c, step), x, y, c))


def first_axis(k):
    return pairs(lambda z, x, y, c: (z, x - k, y, c) if c == 0 else (z, x, y - k, c))


def second_axis(k):
    return pairs(lambda z, x, y, c: (z, x, y - k, c) if c == 0 else (z, x - k, y, c))


def other_core():
    return pairs(lambda z, x, y, c: (z, x, y, 1 - c))


def choose(blocks, owners, messages, place):
    group = lax.axis_index("head")
    core = lax.axis_index("rep") & (NC - 1)
    wide = [blocks[s].astype(jnp.float32) for s in range(NZ)]
    for step, message in enumerate(messages):
        shift = jnp.where(core == 0, z_shift(0, step), z_shift(1, step))
        wanted = (group + shift) & (NZ - 1)
        block = wide[0]
        for s in range(1, NZ):
            block = jnp.where(owners[s : s + 1] == wanted, wide[s], block)
        message[place] = block.astype(jnp.bfloat16)


def prepare_kernel(route, held, *refs):
    messages, rows, other_owners = refs[:STEPS], refs[-2], refs[-1]
    group = lax.axis_index("head")
    replica = lax.axis_index("rep")
    rows[...] = jnp.sum(
        jnp.where(route[:, :, 0, :] == group, route[:, :, 1, :], 0), axis=1
    )
    slots = route[group][:, 0, :]
    lanes = lax.broadcasted_iota(jnp.int32, slots.shape, 1)
    owners = [
        jnp.sum(jnp.where(lanes == source, slots, 0), axis=1, keepdims=True)
        for source in (replica, replica ^ 1)
    ]
    other_owners[...] = jnp.broadcast_to(owners[1], other_owners.shape)
    choose(held, owners[0], messages, 0)


def complete_kernel(swapped, owners, *refs):
    choose(swapped, owners[:, :1], refs[STEPS:], 1)


def prepare(held, route):
    vector = pl.BlockSpec(memory_space=pltpu.VMEM)
    params = pltpu.CompilerParams(vmem_limit_bytes=16 * 2**20)
    message = jax.ShapeDtypeStruct((NC, *held.shape[1:]), held.dtype)
    swapped = move(held, other_core())
    *messages, rows, owners = pl.pallas_call(
        prepare_kernel,
        out_shape=[message] * STEPS
        + [
            jax.ShapeDtypeStruct((NZ, NX * NY * NC), jnp.int32),
            jax.ShapeDtypeStruct((NZ, 128), jnp.int32),
        ],
        in_specs=[vector] * 2,
        out_specs=[vector] * (STEPS + 2),
        compiler_params=params,
    )(route.transpose(0, 2, 3, 1), held)
    messages = pl.pallas_call(
        complete_kernel,
        out_shape=[message] * STEPS,
        in_specs=[vector] * (STEPS + 2),
        out_specs=[vector] * STEPS,
        input_output_aliases={2 + step: step for step in range(STEPS)},
        compiler_params=params,
    )(swapped, owners, *messages)
    return messages, rows


def absorb_kernel(*refs):
    far_rows, own_line, other_line = refs[:3]
    own = refs[3:6]
    other = refs[6:9]
    values, scales, rows, placed, scaled, tables, sems, scale_sem, row_sem = refs[9:]
    at_z = lax.axis_index("head")
    replica = lax.axis_index("rep")
    core = replica & (NC - 1)
    at_x = replica // (NY * NC)
    at_y = (replica // NC) & (NY - 1)
    fetch = pltpu.make_async_copy(far_rows, rows, row_sem)
    fetch.start()
    fetch.wait()
    for arrays, holder in (((own_line, *own), core), ((other_line, *other), 1 - core)):
        planes = []
        for step in range(STEPS):
            ahead = step if step else NZ // 2
            planes.append((at_z + jnp.where(holder == 0, NZ - step, ahead)) & (NZ - 1))
        for second in range(NX):

            def body(first, carry, second=second, planes=planes):
                x = (at_x + jnp.where(holder == 0, first, second)) & (NX - 1)
                y = (at_y + jnp.where(holder == 0, second, first)) & (NY - 1)
                at = x * (NY * NC) + y * NC
                for step in range(STEPS):
                    for i in range(NC):
                        row = pl.multiple_of(rows[planes[step], at + (holder ^ i)], 8)
                        index = first * (STEPS * NC) + step * NC + i
                        block = arrays[second][index].astype(jnp.float32)
                        for h in range(H_DEV):
                            placed[h, pl.ds(row, 8), :] = block[:, h * DH : (h + 1) * DH]
                return carry

            lax.fori_loop(0, NX, body, 0)

    def writes(h, k):
        at = pl.ds(k * SEND * QB, SEND * QB)
        return pltpu.make_async_copy(scaled.at[h, at], values.at[h, at], sems.at[h, k])

    row_at = lax.broadcasted_iota(jnp.int32, (K_BLOCKS, 128), 0)
    col_at = lax.broadcasted_iota(jnp.int32, (K_BLOCKS, 128), 1)
    for h in range(H_DEV):
        key = placed[h, QR:, :].astype(jnp.bfloat16)
        table = jnp.zeros((K_BLOCKS, 128), jnp.float32)
        for i in range(Q_BLOCKS):
            query = placed[h, i * QB : (i + 1) * QB, :].astype(jnp.bfloat16)
            product = lax.dot_general(
                query, key, (((1,), (1,)), ((), ())), preferred_element_type=jnp.float32
            )
            peaks = jnp.max(jnp.abs(product), axis=0, keepdims=True)
            for j in range(K_BLOCKS):
                cols = slice(j * QB, (j + 1) * QB)
                peak = jnp.max(peaks[:, cols], axis=1, keepdims=True)
                scale = (peak + EPSILON).astype(jnp.bfloat16).astype(jnp.float32)
                scaled[h, i * QB : (i + 1) * QB, cols] = (
                    product[:, cols] * (1.0 / scale)
                ).astype(jnp.bfloat16)
                table = jnp.where((row_at == j) & (col_at == i), scale, table)
            if (i + 1) % SEND == 0:
                writes(h, i // SEND).start()
        tables[h] = table[:, :Q_BLOCKS].astype(jnp.bfloat16)
    finish = pltpu.make_async_copy(tables, scales, scale_sem)
    finish.start()
    for h in range(H_DEV):
        for k in range(Q_BLOCKS // SEND):
            writes(h, k).wait()
    finish.wait()


def absorb(rows, own_line, other_line, own, other):
    vector = pl.BlockSpec(memory_space=pltpu.VMEM)
    anywhere = pl.BlockSpec(memory_space=pl.ANY)
    return pl.pallas_call(
        absorb_kernel,
        out_shape=(
            jax.ShapeDtypeStruct((H_DEV, QR, KR), jnp.bfloat16),
            jax.ShapeDtypeStruct((H_DEV, K_BLOCKS, Q_BLOCKS), jnp.bfloat16),
        ),
        in_specs=[vector] * (3 + len(own) + len(other)),
        out_specs=(anywhere, anywhere),
        scratch_shapes=[
            pltpu.SMEM(rows.shape, rows.dtype),
            pltpu.VMEM((H_DEV, LAT, DH), jnp.float32),
            pltpu.VMEM((H_DEV, QR, KR), jnp.bfloat16),
            pltpu.VMEM((H_DEV, K_BLOCKS, Q_BLOCKS), jnp.bfloat16),
            pltpu.SemaphoreType.DMA((H_DEV, Q_BLOCKS // SEND)),
            pltpu.SemaphoreType.DMA,
            pltpu.SemaphoreType.DMA,
        ],
        compiler_params=pltpu.CompilerParams(vmem_limit_bytes=32 * 2**20),
        cost_estimate=pl.CostEstimate(
            flops=2 * H_DEV * QR * KR * DH,
            bytes_accessed=H_DEV * QR * KR * 2,
            transcendentals=0,
        ),
    )(rows, own_line, other_line, *own, *other)


def move(block, target):
    return lax.ppermute(block, AXES, target)


def gather_phase(block, target):
    return [block] + [lax.ppermute(block, AXES, target(k)) for k in (1, 2, 3)]


def on_device(trainer_rows, route):
    messages, rows = prepare(trainer_rows[0, 0], route)
    arrived = jnp.concatenate(
        [lax.ppermute(m, AXES, along_z(s)) for s, m in enumerate(messages)]
    )
    line = jnp.concatenate(gather_phase(arrived, first_axis))
    own = [move(line, second_axis(k)) for k in (1, 2, 3)]
    other = [move(piece, other_core()) for piece in own]
    other_line = move(line, other_core())
    values, scales = absorb(rows, line, other_line, own, other)
    return values, scales.transpose(0, 2, 1)


def solution(mesh):
    return jax.shard_map(
        on_device,
        mesh=mesh,
        in_specs=(P("head", "rep", None, None, None), P()),
        out_specs=(P("head", None, None), P("head", None, None)),
        check_vma=False,
    )
```

```python
import jax
import jax.numpy as jnp
from jax import lax
from jax.experimental import pallas as pl
from jax.experimental.pallas import tpu as pltpu
from jax.sharding import PartitionSpec as P

QR = 1536
KR = 512
DH = 128
H_DEV = 8
QB = 128
LAT = QR + KR
NZ = 8
NX = 4
NY = 4
NC = 2
STEPS = NZ // NC
Q_BLOCKS = QR // QB
K_BLOCKS = KR // QB
SEND = 4
HALF = H_DEV // 2
WIDE = HALF * DH
ORDER = (1, 3, 2)
EARLY = (0, 2, 3)
LATE = 1
EPSILON = 1e-06
AXES = ("head", "rep")


def index_of(z, x, y, c):
    return (z % NZ) * (NX * NY * NC) + (x % NX) * (NY * NC) + (y % NY) * NC + c


def pairs(target):
    every = [
        (z, x, y, c)
        for z in range(NZ)
        for x in range(NX)
        for y in range(NY)
        for c in range(NC)
    ]
    return [(index_of(*d), index_of(*target(*d))) for d in every]


def z_shift(core, step):
    if core == 0:
        return step
    return -step if step else NZ // 2


def along_z(step):
    return pairs(lambda z, x, y, c: (z + z_shift(c, step), x, y, c))


def first_axis(k):
    return pairs(lambda z, x, y, c: (z, x - k, y, c) if c == 0 else (z, x, y - k, c))


def second_axis(k):
    return pairs(lambda z, x, y, c: (z, x, y - k, c) if c == 0 else (z, x - k, y, c))


def other_core():
    return pairs(lambda z, x, y, c: (z, x, y, 1 - c))


def choose(blocks, owners, messages, place):
    group = lax.axis_index("head")
    core = lax.axis_index("rep") & (NC - 1)
    wide = [blocks[s].astype(jnp.float32) for s in range(NZ)]
    for step, message in enumerate(messages):
        shift = jnp.where(core == 0, z_shift(0, step), z_shift(1, step))
        wanted = (group + shift) & (NZ - 1)
        block = wide[0]
        for s in range(1, NZ):
            block = jnp.where(owners[s : s + 1] == wanted, wide[s], block)
        message[place] = block.astype(jnp.bfloat16)


def prepare_kernel(route, held, *refs):
    messages, rows, other_owners = refs[:STEPS], refs[-2], refs[-1]
    group = lax.axis_index("head")
    replica = lax.axis_index("rep")
    rows[...] = jnp.sum(
        jnp.where(route[:, :, 0, :] == group, route[:, :, 1, :], 0), axis=1
    )
    slots = route[group][:, 0, :]
    lanes = lax.broadcasted_iota(jnp.int32, slots.shape, 1)
    owners = [
        jnp.sum(jnp.where(lanes == source, slots, 0), axis=1, keepdims=True)
        for source in (replica, replica ^ 1)
    ]
    other_owners[...] = jnp.broadcast_to(owners[1], other_owners.shape)
    choose(held, owners[0], messages, 0)


def complete_kernel(swapped, owners, *refs):
    choose(swapped, owners[:, :1], refs[STEPS:], 1)


def prepare(held, route):
    vector = pl.BlockSpec(memory_space=pltpu.VMEM)
    params = pltpu.CompilerParams(vmem_limit_bytes=16 * 2**20)
    message = jax.ShapeDtypeStruct((NC, *held.shape[1:]), held.dtype)
    swapped = move(held, other_core())
    *messages, rows, owners = pl.pallas_call(
        prepare_kernel,
        out_shape=[message] * STEPS
        + [
            jax.ShapeDtypeStruct((NZ, NX * NY * NC), jnp.int32),
            jax.ShapeDtypeStruct((NZ, 128), jnp.int32),
        ],
        in_specs=[vector] * 2,
        out_specs=[vector] * (STEPS + 2),
        compiler_params=params,
    )(route.transpose(0, 2, 3, 1), held)
    messages = pl.pallas_call(
        complete_kernel,
        out_shape=[message] * STEPS,
        in_specs=[vector] * (STEPS + 2),
        out_specs=[vector] * STEPS,
        input_output_aliases={2 + step: step for step in range(STEPS)},
        compiler_params=params,
    )(swapped, owners, *messages)
    return messages, rows


def place_blocks(rows, pieces, placed):
    at_z = lax.axis_index("head")
    replica = lax.axis_index("rep")
    core = replica & (NC - 1)
    at_x = replica // (NY * NC)
    at_y = (replica // NC) & (NY - 1)

    def place(first, carry):
        for blocks, second, mine in pieces:
            holder = core if mine else 1 - core
            x = (at_x + jnp.where(holder == 0, first, second)) & (NX - 1)
            y = (at_y + jnp.where(holder == 0, second, first)) & (NY - 1)
            at = x * (NY * NC) + y * NC
            for step in range(STEPS):
                z = at_z - jnp.where(holder == 0, z_shift(0, step), z_shift(1, step))
                for i in range(NC):
                    row = pl.multiple_of(rows[z & (NZ - 1), at + (holder ^ i)], 8)
                    index = first * (STEPS * NC) + step * NC + i
                    block = blocks[index].astype(jnp.float32)
                    for h in range(H_DEV):
                        placed[h, pl.ds(row, 8), :] = block[:, h * DH : (h + 1) * DH]
        return carry

    lax.fori_loop(0, NX, place, 0)


def fetch_rows(far_rows, rows, sem):
    fetch = pltpu.make_async_copy(far_rows, rows, sem)
    fetch.start()
    fetch.wait()


def place_kernel(far_rows, *refs):
    own, other, (placed, rows, row_sem) = refs[:4], refs[4:-3], refs[-3:]
    fetch_rows(far_rows, rows, row_sem)
    pieces = [(blocks, second, True) for second, blocks in zip((0, *ORDER), own, strict=True)]
    pieces += [(blocks, second, False) for second, blocks in zip(EARLY, other, strict=True)]
    place_blocks(rows, pieces, placed)


def absorb_kernel(far_rows, late, early, values, scales, placed, rows, scaled, tables, *sems):
    value_sems, scale_sem, row_sem = sems
    fetch_rows(far_rows, rows, row_sem)
    place_blocks(rows, [(late, LATE, False)], placed)

    def writes(h, k):
        at = pl.ds(k * SEND * QB, SEND * QB)
        return pltpu.make_async_copy(
            scaled.at[h, at], values.at[h, at], value_sems.at[h, k]
        )

    row_at = lax.broadcasted_iota(jnp.int32, (K_BLOCKS, 128), 0)
    col_at = lax.broadcasted_iota(jnp.int32, (K_BLOCKS, 128), 1)
    for h in range(H_DEV):
        key = placed[h, QR:, :].astype(jnp.bfloat16)
        table = jnp.zeros((K_BLOCKS, 128), jnp.float32)
        for i in range(Q_BLOCKS):
            query = placed[h, i * QB : (i + 1) * QB, :].astype(jnp.bfloat16)
            product = lax.dot_general(
                query, key, (((1,), (1,)), ((), ())), preferred_element_type=jnp.float32
            )
            peaks = jnp.max(jnp.abs(product), axis=0, keepdims=True)
            for j in range(K_BLOCKS):
                cols = slice(j * QB, (j + 1) * QB)
                peak = jnp.max(peaks[:, cols], axis=1, keepdims=True)
                scale = (peak + EPSILON).astype(jnp.bfloat16).astype(jnp.float32)
                scaled[h, i * QB : (i + 1) * QB, cols] = (
                    product[:, cols] * (1.0 / scale)
                ).astype(jnp.bfloat16)
                table = jnp.where((row_at == j) & (col_at == i), scale, table)
            if (i + 1) % SEND == 0:
                writes(h, i // SEND).start()
        tables[h] = table[:, :Q_BLOCKS].astype(jnp.bfloat16)
    finish = pltpu.make_async_copy(tables, scales, scale_sem)
    finish.start()
    for h in range(H_DEV):
        for k in range(Q_BLOCKS // SEND):
            writes(h, k).wait()
    finish.wait()


def absorb(rows, own, other):
    vector = pl.BlockSpec(memory_space=pltpu.VMEM)
    anywhere = pl.BlockSpec(memory_space=pl.ANY)
    placed = jax.ShapeDtypeStruct((H_DEV, LAT, DH), jnp.float32)
    fetched = [pltpu.SMEM(rows.shape, rows.dtype)]
    early = pl.pallas_call(
        place_kernel,
        out_shape=placed,
        in_specs=[vector] * (1 + NX + len(EARLY)),
        out_specs=vector,
        scratch_shapes=[*fetched, pltpu.SemaphoreType.DMA],
        compiler_params=pltpu.CompilerParams(vmem_limit_bytes=4 * 2**20),
    )(rows, *own.values(), *[other[k] for k in EARLY])
    values, scales, _ = pl.pallas_call(
        absorb_kernel,
        out_shape=(
            jax.ShapeDtypeStruct((H_DEV, QR, KR), jnp.bfloat16),
            jax.ShapeDtypeStruct((H_DEV, K_BLOCKS, Q_BLOCKS), jnp.bfloat16),
            placed,
        ),
        in_specs=[vector] * 3,
        out_specs=(anywhere, anywhere, vector),
        scratch_shapes=[
            *fetched,
            pltpu.VMEM((H_DEV, QR, KR), jnp.bfloat16),
            pltpu.VMEM((H_DEV, K_BLOCKS, Q_BLOCKS), jnp.bfloat16),
            pltpu.SemaphoreType.DMA((H_DEV, Q_BLOCKS // SEND)),
            pltpu.SemaphoreType.DMA,
            pltpu.SemaphoreType.DMA,
        ],
        input_output_aliases={2: 2},
        compiler_params=pltpu.CompilerParams(vmem_limit_bytes=20 * 2**20),
        cost_estimate=pl.CostEstimate(
            flops=2 * H_DEV * QR * KR * DH,
            bytes_accessed=H_DEV * QR * KR * 2,
            transcendentals=0,
        ),
    )(rows, other[LATE], early)
    return values, scales


def move(block, target):
    return lax.ppermute(block, AXES, target)


def gather_phase(block, target):
    return [block] + [lax.ppermute(block, AXES, target(k)) for k in (1, 2, 3)]


def on_device(trainer_rows, route):
    messages, rows = prepare(trainer_rows[0, 0], route)
    arrived = jnp.concatenate(
        [lax.ppermute(m, AXES, along_z(s)) for s, m in enumerate(messages)]
    )
    line = jnp.concatenate(gather_phase(arrived, first_axis))
    own = {0: line} | {k: move(line, second_axis(k)) for k in ORDER}
    other = {k: move(piece, other_core()) for k, piece in own.items()}
    values, scales = absorb(rows, own, other)
    return values, scales.transpose(0, 2, 1)


def solution(mesh):
    return jax.shard_map(
        on_device,
        mesh=mesh,
        in_specs=(P("head", "rep", None, None, None), P()),
        out_specs=(P("head", None, None), P("head", None, None)),
        check_vma=False,
    )
```

```python
import jax
import jax.numpy as jnp
from jax import lax
from jax.experimental import pallas as pl
from jax.experimental.pallas import tpu as pltpu
from jax.sharding import PartitionSpec as P

QR = 1536
KR = 512
DH = 128
H_DEV = 8
QB = 128
LAT = QR + KR
NZ = 8
NX = 4
NY = 4
NC = 2
STEPS = NZ // NC
Q_BLOCKS = QR // QB
K_BLOCKS = KR // QB
SEND = 4
HALF = H_DEV // 2
WIDE = HALF * DH
ORDER = (1, 3, 2)
EARLY = (0, 2, 3)
LATE = 1
EPSILON = 1e-06
AXES = ("head", "rep")


def index_of(z, x, y, c):
    return (z % NZ) * (NX * NY * NC) + (x % NX) * (NY * NC) + (y % NY) * NC + c


def pairs(target):
    every = [
        (z, x, y, c)
        for z in range(NZ)
        for x in range(NX)
        for y in range(NY)
        for c in range(NC)
    ]
    return [(index_of(*d), index_of(*target(*d))) for d in every]


def z_shift(core, step):
    if core == 0:
        return step
    return -step if step else NZ // 2


def along_z(step):
    return pairs(lambda z, x, y, c: (z + z_shift(c, step), x, y, c))


def first_axis(k):
    return pairs(lambda z, x, y, c: (z, x - k, y, c) if c == 0 else (z, x, y - k, c))


def second_axis(k):
    return pairs(lambda z, x, y, c: (z, x, y - k, c) if c == 0 else (z, x - k, y, c))


def other_core():
    return pairs(lambda z, x, y, c: (z, x, y, 1 - c))


def choose(blocks, owners, messages, place):
    group = lax.axis_index("head")
    core = lax.axis_index("rep") & (NC - 1)
    wide = [blocks[s].astype(jnp.float32) for s in range(NZ)]
    for step, message in enumerate(messages):
        shift = jnp.where(core == 0, z_shift(0, step), z_shift(1, step))
        wanted = (group + shift) & (NZ - 1)
        block = wide[0]
        for s in range(1, NZ):
            block = jnp.where(owners[s : s + 1] == wanted, wide[s], block)
        message[place] = block.astype(jnp.bfloat16)


def prepare_kernel(route, held, *refs):
    messages, rows, other_owners = refs[:STEPS], refs[-2], refs[-1]
    group = lax.axis_index("head")
    replica = lax.axis_index("rep")
    rows[...] = jnp.sum(
        jnp.where(route[:, :, 0, :] == group, route[:, :, 1, :], 0), axis=1
    )
    slots = route[group][:, 0, :]
    lanes = lax.broadcasted_iota(jnp.int32, slots.shape, 1)
    owners = [
        jnp.sum(jnp.where(lanes == source, slots, 0), axis=1, keepdims=True)
        for source in (replica, replica ^ 1)
    ]
    other_owners[...] = jnp.broadcast_to(owners[1], other_owners.shape)
    choose(held, owners[0], messages, 0)


def complete_kernel(swapped, owners, *refs):
    choose(swapped, owners[:, :1], refs[STEPS:], 1)


def prepare(held, route):
    vector = pl.BlockSpec(memory_space=pltpu.VMEM)
    params = pltpu.CompilerParams(vmem_limit_bytes=16 * 2**20)
    message = jax.ShapeDtypeStruct((NC, *held.shape[1:]), held.dtype)
    swapped = move(held, other_core())
    *messages, rows, owners = pl.pallas_call(
        prepare_kernel,
        out_shape=[message] * STEPS
        + [
            jax.ShapeDtypeStruct((NZ, NX * NY * NC), jnp.int32),
            jax.ShapeDtypeStruct((NZ, 128), jnp.int32),
        ],
        in_specs=[vector] * 2,
        out_specs=[vector] * (STEPS + 2),
        compiler_params=params,
    )(route.transpose(0, 2, 3, 1), held)
    messages = pl.pallas_call(
        complete_kernel,
        out_shape=[message] * STEPS,
        in_specs=[vector] * (STEPS + 2),
        out_specs=[vector] * STEPS,
        input_output_aliases={2 + step: step for step in range(STEPS)},
        compiler_params=params,
    )(swapped, owners, *messages)
    return messages, rows


def place_blocks(rows, pieces, placed):
    at_z = lax.axis_index("head")
    replica = lax.axis_index("rep")
    core = replica & (NC - 1)
    at_x = replica // (NY * NC)
    at_y = (replica // NC) & (NY - 1)

    def place(first, carry):
        offset = (NX - first) & (NX - 1)
        for blocks, second, mine in pieces:
            holder = core if mine else 1 - core
            x = (at_x + jnp.where(holder == 0, offset, second)) & (NX - 1)
            y = (at_y + jnp.where(holder == 0, second, offset)) & (NY - 1)
            at = x * (NY * NC) + y * NC
            for step in range(STEPS):
                z = at_z - jnp.where(holder == 0, z_shift(0, step), z_shift(1, step))
                for i in range(NC):
                    row = pl.multiple_of(rows[z & (NZ - 1), at + (holder ^ i)], 8)
                    index = first * (STEPS * NC) + step * NC + i
                    block = blocks[index].astype(jnp.float32)
                    for h in range(H_DEV):
                        placed[h, pl.ds(row, 8), :] = block[:, h * DH : (h + 1) * DH]
        return carry

    lax.fori_loop(0, NX, place, 0)


def fetch_rows(far_rows, rows, sem):
    fetch = pltpu.make_async_copy(far_rows, rows, sem)
    fetch.start()
    fetch.wait()


def place_kernel(far_rows, *refs):
    own, other, (placed, rows, row_sem) = refs[:4], refs[4:-3], refs[-3:]
    fetch_rows(far_rows, rows, row_sem)
    pieces = [(blocks, second, True) for second, blocks in zip((0, *ORDER), own, strict=True)]
    pieces += [(blocks, second, False) for second, blocks in zip(EARLY, other, strict=True)]
    place_blocks(rows, pieces, placed)


def absorb_kernel(far_rows, late, early, values, scales, placed, rows, scaled, tables, *sems):
    value_sems, scale_sem, row_sem = sems
    fetch_rows(far_rows, rows, row_sem)
    place_blocks(rows, [(late, LATE, False)], placed)

    def writes(h, k):
        at = pl.ds(k * SEND * QB, SEND * QB)
        return pltpu.make_async_copy(
            scaled.at[h, at], values.at[h, at], value_sems.at[h, k]
        )

    row_at = lax.broadcasted_iota(jnp.int32, (K_BLOCKS, 128), 0)
    col_at = lax.broadcasted_iota(jnp.int32, (K_BLOCKS, 128), 1)
    for h in range(H_DEV):
        key = placed[h, QR:, :].astype(jnp.bfloat16)
        table = jnp.zeros((K_BLOCKS, 128), jnp.float32)
        for i in range(Q_BLOCKS):
            query = placed[h, i * QB : (i + 1) * QB, :].astype(jnp.bfloat16)
            product = lax.dot_general(
                query, key, (((1,), (1,)), ((), ())), preferred_element_type=jnp.float32
            )
            peaks = jnp.max(jnp.abs(product), axis=0, keepdims=True)
            for j in range(K_BLOCKS):
                cols = slice(j * QB, (j + 1) * QB)
                peak = jnp.max(peaks[:, cols], axis=1, keepdims=True)
                scale = (peak + EPSILON).astype(jnp.bfloat16).astype(jnp.float32)
                scaled[h, i * QB : (i + 1) * QB, cols] = (
                    product[:, cols] * (1.0 / scale)
                ).astype(jnp.bfloat16)
                table = jnp.where((row_at == j) & (col_at == i), scale, table)
            if (i + 1) % SEND == 0:
                writes(h, i // SEND).start()
        tables[h] = table[:, :Q_BLOCKS].astype(jnp.bfloat16)
    finish = pltpu.make_async_copy(tables, scales, scale_sem)
    finish.start()
    for h in range(H_DEV):
        for k in range(Q_BLOCKS // SEND):
            writes(h, k).wait()
    finish.wait()


def absorb(rows, own, other):
    vector = pl.BlockSpec(memory_space=pltpu.VMEM)
    anywhere = pl.BlockSpec(memory_space=pl.ANY)
    placed = jax.ShapeDtypeStruct((H_DEV, LAT, DH), jnp.float32)
    fetched = [pltpu.SMEM(rows.shape, rows.dtype)]
    early = pl.pallas_call(
        place_kernel,
        out_shape=placed,
        in_specs=[vector] * (1 + NX + len(EARLY)),
        out_specs=vector,
        scratch_shapes=[*fetched, pltpu.SemaphoreType.DMA],
        compiler_params=pltpu.CompilerParams(vmem_limit_bytes=4 * 2**20),
    )(rows, *own.values(), *[other[k] for k in EARLY])
    values, scales, _ = pl.pallas_call(
        absorb_kernel,
        out_shape=(
            jax.ShapeDtypeStruct((H_DEV, QR, KR), jnp.bfloat16),
            jax.ShapeDtypeStruct((H_DEV, K_BLOCKS, Q_BLOCKS), jnp.bfloat16),
            placed,
        ),
        in_specs=[vector] * 3,
        out_specs=(anywhere, anywhere, vector),
        scratch_shapes=[
            *fetched,
            pltpu.VMEM((H_DEV, QR, KR), jnp.bfloat16),
            pltpu.VMEM((H_DEV, K_BLOCKS, Q_BLOCKS), jnp.bfloat16),
            pltpu.SemaphoreType.DMA((H_DEV, Q_BLOCKS // SEND)),
            pltpu.SemaphoreType.DMA,
            pltpu.SemaphoreType.DMA,
        ],
        input_output_aliases={2: 2},
        compiler_params=pltpu.CompilerParams(vmem_limit_bytes=20 * 2**20),
        cost_estimate=pl.CostEstimate(
            flops=2 * H_DEV * QR * KR * DH,
            bytes_accessed=H_DEV * QR * KR * 2,
            transcendentals=0,
        ),
    )(rows, other[LATE], early)
    return values, scales


def move(block, target):
    return lax.ppermute(block, AXES, target)


def on_device(trainer_rows, route):
    messages, rows = prepare(trainer_rows[0, 0], route)
    arrived = jnp.concatenate(
        [lax.ppermute(m, AXES, along_z(s)) for s, m in enumerate(messages)]
    )
    line = jnp.concatenate([arrived] + [move(arrived, first_axis(k)) for k in (3, 2, 1)])
    own = {0: line} | {k: move(line, second_axis(k)) for k in ORDER}
    other = {k: move(piece, other_core()) for k, piece in own.items()}
    values, scales = absorb(rows, own, other)
    return values, scales.transpose(0, 2, 1)


def solution(mesh):
    return jax.shard_map(
        on_device,
        mesh=mesh,
        in_specs=(P("head", "rep", None, None, None), P()),
        out_specs=(P("head", None, None), P("head", None, None)),
        check_vma=False,
    )
```
